32 devices in a mesh: groups: 2 (over x), pool: 16 (over z, y, core).
Axes of the slice: x: 2, y: 2, z: 4, core: 2. Of those that a mesh axis runs over, the one named last changes fastest.
Arguments:
- query_rows: bfloat16 [4096, 8192], P(('groups', 'pool')), parts along dimension 0, may hold values from -125 to 125
- suffix_kv: bfloat16 [4096, 2048], P(('groups', 'pool')), parts along dimension 0, may hold values from -7 to 7
- delta_codes: int32 [256, 16, 2048], P(('groups', 'pool')), parts along dimension 0, may hold values from -127 to 127
- anchors: bfloat16 [256, 2048], P(('groups', 'pool')), parts along dimension 0, may hold values from -6 to 6
- scales: float32 [256, 16], P(('groups', 'pool')), parts along dimension 0, may hold values from 0.001 to 0.01
- anchor_pos: int32 [256], P(('groups', 'pool')), parts along dimension 0, may hold values from 0 to 15
- hit_slot: int32 [64, 1], P('groups'), parts along dimension 0, may hold values from 0 to 7
- hit_owner: int32 [64, 1], P('groups'), parts along dimension 0, may hold values from 0 to 15; in each aligned block of 32 rows (0 to 31, 32 to 63, ...) at most 6 rows name the same one
Outputs:
- context: bfloat16 [4096, 8192], P(('groups', 'pool')), parts along dimension 0
The draws below stay inside these ranges and needn't reach their ends.
There are 2 independent parts, one for each index of `groups`. The reference program is written for one: setup_inputs(seed, part) draws one part's arguments, and reference() takes and returns one part's arrays. A program takes and returns all parts, laid end to end along the dimension named above; each array names one. Nothing has to cross between parts.
Inputs may be any that keep to these rules, and one draw needn't show every extreme that they name: `hit_owner`: each pool device stores at most 6 of the 32 prefix pages, and some device stores exactly 6.
All inputs are finite; a program needn't handle non-finite values.
Results may differ from the reference program's by a relative error of at most 0.0045.
Values may be sent and summed in bfloat16 or wider, within the bound.
A program may use at most 448 MiB of HBM per device.

```python
import math
import jax
import jax.numpy as jnp
import numpy as np
from jax import lax

H = 64
KVH = 8
HD = 128
PAGE = 16
STORE_DEV = 8
MOST = 6
NPAGE = 32
SUFFIX = 2048
STORE_ALL = 128
N_POOL = 16


def shared_keys(key, lifted):
    base = jnp.clip(jax.random.normal(key, (SUFFIX, KVH * HD), jnp.float32), -6.0, 6.0)
    rows_all = jnp.arange(SUFFIX)
    chosen = (rows_all % 64 == 1) & (lifted > 0.0)
    earlier = jnp.roll(base, 1, axis=0)
    moved = jnp.where(chosen[:, None], 1.01 * earlier, base)
    return (base, moved, chosen)


def draw_suffix_kv(key, part):
    lifted = 0.0
    base, moved, chosen = shared_keys(key, lifted)
    key = jax.random.fold_in(key, 7)
    values_part = jnp.clip(jax.random.normal(key, (SUFFIX, KVH * HD), jnp.float32), -6.0, 6.0)
    return jnp.concatenate([moved, values_part], axis=1).astype(jnp.bfloat16)


def draw_query_rows(key, part):
    lifted = 0.0
    base, moved, chosen = shared_keys(key, lifted)
    key = jax.random.fold_in(key, 11)
    drawn = jnp.clip(jax.random.normal(key, (SUFFIX, KVH, H // KVH, HD), jnp.float32), -6.0, 6.0)
    rows_all = jnp.arange(SUFFIX)
    strength = (10.0 + 5.0 * (rows_all // 64 % 3)).astype(jnp.float32)
    earlier = jnp.roll(base, 1, axis=0).reshape(SUFFIX, KVH, 1, HD)
    aligned = strength[:, None, None, None] * jnp.broadcast_to(earlier, drawn.shape)
    result = jnp.where(chosen[:, None, None, None], aligned, drawn)
    return result.reshape(SUFFIX, H * HD).astype(jnp.bfloat16)


def with_ends(entries, key, least, largest):
    extent = entries.shape
    place = [jax.random.randint(jax.random.fold_in(key, axis), (), 0, extent[axis]) for axis in range(len(extent))]
    entries = entries.at[tuple(place)].set(least)
    longest = extent.index(max(extent))
    place[longest] = (place[longest] + 1) % extent[longest]
    return entries.at[tuple(place)].set(largest)


def levels(stream_key, shape, cuts, smallest, high):
    def one(axis_at, parts):
        heights = jax.random.uniform(jax.random.fold_in(jax.random.fold_in(stream_key, 6), axis_at), (parts,), jnp.float32, smallest / len(cuts), high / len(cuts))
        return jnp.repeat(jnp.exp(heights), shape[axis_at] // parts).reshape((-1,) + (1,) * (len(shape) - axis_at - 1))

    loudness = one(*cuts[0])
    for cut in cuts[1:]:
        loudness = loudness * one(*cut)
    return loudness


def routed_block(own_key, own, number, rows, amount, top, limit, skew):
    order = jax.random.permutation(own_key, amount)
    packed, usual = portions_of(amount, rows * top, limit, skew, True), portions_of(amount, rows * top, limit, skew, False)
    places = jnp.arange(amount)

    def named(sizes, rotation):
        used = int((sizes > 0).sum())
        fixed = max(1, used // 4)
        moved = fixed + (places - fixed + rotation * (used - fixed)) % max(1, amount - fixed)
        return jnp.zeros((amount,), jnp.int32).at[order[jnp.where(places < fixed, places, moved)]].set(jnp.asarray(sizes, jnp.int32))

    sizes = jnp.where(number % 4 == 0, named(packed, number // 4), named(usual, number - number // 4 - 1))
    mixed = jax.random.permutation(jax.random.fold_in(own, 3), amount)
    giver, sink = mixed[0:amount // 2 * 2:2], mixed[1:amount // 2 * 2:2]
    slack = jnp.minimum(sizes[giver] - 1, limit - sizes[sink]) // 2
    slack = jnp.where((giver == order[0]) | (sink == order[0]) | (sizes[sink] == 0), 0, jnp.maximum(slack, 0))
    moved = jax.random.randint(jax.random.fold_in(own, 4), (amount // 2,), 0, 1 << 20) % (slack + 1)
    sizes = sizes.at[giver].add(-moved).at[sink].add(moved)
    items = jnp.searchsorted(jnp.cumsum(sizes), jnp.arange(rows * top), side="right").astype(jnp.int32)
    listing = items.reshape(top, rows).T
    listing = listing[jax.random.permutation(jax.random.fold_in(own, 1), rows)]
    rotation = jax.random.randint(jax.random.fold_in(own, 2), (rows, 1), 0, top)
    return jnp.take_along_axis(listing, (jnp.arange(top)[None, :] + rotation) % top, axis=1)


def portions_of(amount, total, bound, lean, full):
    weights = [(1 << 20) // math.isqrt(standing ** lean) + 1 for standing in range(1, amount + 1)]
    largest = bound if full else min(bound, max(-(-total // amount), total * weights[0] // sum(weights)))
    least = 1 if total - largest >= amount - 1 else 0
    given, surplus = [largest] + [least] * (amount - 1), total - largest - least * (amount - 1)
    while surplus > 0:
        free = [i for i in range(1, amount) if given[i] < largest] or [i for i in range(1, amount) if given[i] < bound]
        whole, remaining = sum([weights[i] for i in free]), surplus
        for i in free:
            extra = min(bound - given[i], max(1, remaining * weights[i] // whole), surplus)
            given[i] = given[i] + extra
            surplus = surplus - extra
    return np.array(given)


def bell_draw(key, extent, scale, limit, shards=(), kind=jnp.bfloat16):
    loudness = levels(key, extent, shards, -0.22, 0.18) if shards else 1.0
    entries = jax.random.normal(key, extent, jnp.float32) * scale * loudness
    return jnp.minimum(jnp.maximum(entries, -limit), limit).astype(kind)


def setup_inputs(seed: int = 0, part: int = 0) -> dict:
    key_list = jax.random.split(jax.random.key(seed), 9)
    part_keys = jax.random.split(jax.random.fold_in(key_list[8], part), 9)
    query_rows = draw_query_rows(jax.random.fold_in(jax.random.fold_in(key_list[8], part), 71), part)
    suffix_kv = draw_suffix_kv(jax.random.fold_in(jax.random.fold_in(key_list[8], part), 71), part)
    delta_codes = with_ends(jax.random.randint(part_keys[2], (STORE_ALL, PAGE, 2 * KVH * HD), -127, 128), jax.random.fold_in(part_keys[2], 1), -127, 127).astype(jnp.int32)
    anchors = bell_draw(part_keys[3], (STORE_ALL, 2 * KVH * HD), 1.0, 6.0, ((0, 16),))
    scales = jnp.clip(jnp.exp(math.log(0.01) - 2.30258502 * jax.random.uniform(part_keys[4], (STORE_ALL, 2 * KVH), jnp.float32) ** levels(part_keys[4], (STORE_ALL, 2 * KVH), ((0, 16),), -0.2, 0.2)), 0.001, 0.01)
    anchor_pos = with_ends(jax.random.randint(part_keys[5], (STORE_ALL,), 0, PAGE), jax.random.fold_in(part_keys[5], 1), 0, PAGE - 1).astype(jnp.int32)
    hit_slot = with_ends(jax.random.randint(part_keys[6], (NPAGE, 1), 0, STORE_DEV), jax.random.fold_in(part_keys[6], 1), 0, STORE_DEV - 1).astype(jnp.int32)
    hit_owner_keys = jax.random.split(jax.random.fold_in(part_keys[7], 1), NPAGE // NPAGE)
    hit_owner_turns = jax.random.permutation(jax.random.fold_in(part_keys[7], 3), NPAGE // NPAGE)
    hit_owner = jax.vmap(lambda own, number: routed_block(jax.random.fold_in(part_keys[7], 2), own, number, NPAGE, N_POOL, 1, MOST, 2))(hit_owner_keys, hit_owner_turns).reshape((NPAGE, 1))
    return {"query_rows": query_rows, "suffix_kv": suffix_kv, "delta_codes": delta_codes, "anchors": anchors, "scales": scales, "anchor_pos": anchor_pos, "hit_slot": hit_slot, "hit_owner": hit_owner}


def expand_pages(page_codes, page_anchor, page_scale, page_anchor_pos):
    page_len = page_codes.shape[1]
    head_dim = page_codes.shape[2] // page_scale.shape[1]
    triangle = (jnp.arange(page_len)[None, :] <= jnp.arange(page_len)[:, None]).astype(jnp.float32)
    anchor_row = jnp.take(triangle, page_anchor_pos.astype(jnp.int32), axis=0)
    mixing = triangle[None, :, :] - anchor_row[:, None, :]
    summed = jnp.einsum("pts,psc->ptc", mixing, page_codes.astype(jnp.float32), precision=lax.Precision.HIGHEST)
    widened = jnp.repeat(page_scale.astype(jnp.float32), head_dim, axis=1)
    return (page_anchor.astype(jnp.float32)[:, None, :] + widened[:, None, :] * summed).astype(jnp.bfloat16)


def reference(query_rows, suffix_kv, delta_codes, anchors, scales, anchor_pos, hit_slot, hit_owner):
    decoded = expand_pages(delta_codes, anchors, scales, anchor_pos)
    picked = (hit_owner[:, 0] * STORE_DEV + hit_slot[:, 0]).astype(jnp.int32)
    prefix_kv = jnp.take(decoded, picked, axis=0).reshape(NPAGE * PAGE, 2 * KVH * HD)
    all_keys = jnp.concatenate([prefix_kv, suffix_kv], axis=0)
    key_pos = jnp.concatenate([jnp.full((NPAGE * PAGE,), -1, jnp.int32), jnp.arange(SUFFIX, dtype=jnp.int32)])
    query_pos = jnp.arange(SUFFIX, dtype=jnp.int32)
    visible = key_pos[None, :] <= query_pos[:, None]
    head_view = query_rows.reshape(SUFFIX, H, HD)
    score_scale = HD ** -0.5

    def one_head(head):
        group = (head // (H // KVH)).astype(jnp.int32)
        queries = lax.dynamic_index_in_dim(head_view, head, 1, keepdims=False)
        key_cols = lax.dynamic_slice_in_dim(all_keys, group * HD, HD, 1)
        value_cols = lax.dynamic_slice_in_dim(all_keys, KVH * HD + group * HD, HD, 1)
        scores = jnp.dot(queries, key_cols.T, preferred_element_type=jnp.float32) * score_scale
        scores = jnp.where(visible, scores, jnp.float32(-1e30))
        peak = jnp.max(scores, axis=1, keepdims=True)
        weights = jnp.where(visible, jnp.exp(scores - peak), jnp.float32(0.0))
        denom = jnp.sum(weights, axis=1, keepdims=True)
        rounded = weights.astype(jnp.bfloat16)
        mixed = jnp.dot(rounded, value_cols, preferred_element_type=jnp.float32) / denom
        return mixed.astype(jnp.bfloat16)

    stacked = lax.map(one_head, jnp.arange(H, dtype=jnp.int32))
    return jnp.transpose(stacked, (1, 0, 2)).reshape(SUFFIX, H * HD)
```

```python
import functools
import jax
import jax.numpy as jnp
from jax import lax
from jax.experimental import pallas as pl
from jax.experimental.pallas import tpu as pltpu
from jax.sharding import PartitionSpec as P

H = 64
KVH = 8
MOST = 6

LOG2E = 1.4426950408889634


def expand_pages(page_codes, page_anchor, page_scale, page_anchor_pos):
    page_len = page_codes.shape[1]
    head_dim = page_codes.shape[2] // page_scale.shape[1]
    triangle = (jnp.arange(page_len)[None, :] <= jnp.arange(page_len)[:, None]).astype(jnp.float32)
    anchor_row = jnp.take(triangle, page_anchor_pos, axis=0)
    mixing = triangle[None, :, :] - anchor_row[:, None, :]
    summed = jnp.einsum(
        "pts,psc->ptc", mixing, page_codes.astype(jnp.float32), precision=lax.Precision.HIGHEST
    )
    widened = jnp.repeat(page_scale, head_dim, axis=1)
    return (page_anchor.astype(jnp.float32)[:, None, :] + widened[:, None, :] * summed).astype(
        jnp.bfloat16
    )


def local_pages(delta_codes, anchors, scales, anchor_pos, hit_slot, hit_owner, my_index):
    owners = hit_owner[:, 0]
    slot_ids = hit_slot[:, 0]
    mine = (owners == my_index).astype(jnp.int32)
    page_rank = jnp.cumsum(mine) - 1
    buffer_ids = jnp.arange(MOST, dtype=jnp.int32)
    chosen = ((mine[None, :] == 1) & (page_rank[None, :] == buffer_ids[:, None])).astype(jnp.int32)
    picked = jnp.sum(chosen * slot_ids[None, :], axis=1)
    filled = jnp.sum(chosen, axis=1) > 0
    pages_now = expand_pages(
        jnp.take(delta_codes, picked, axis=0),
        jnp.take(anchors, picked, axis=0),
        jnp.take(scales, picked, axis=0),
        jnp.take(anchor_pos, picked, axis=0),
    )
    return (pages_now, filled)


def flash_body(place, pages, q_ref, kp_ref, vp_ref, ks_ref, vs_ref, o_ref, qs, kb, vb, top, tot, acc, *, share, hd, page, npage, tok, blk, rt, wide):
    my = place[0]
    R = share*tok
    c = hd**-0.5*LOG2E
    for h in range(share):
        q=q_ref[:, h*hd:(h+1)*hd]
        if wide:
            qf=q.astype(jnp.float32)*c
            hi=qf.astype(jnp.bfloat16)
            qs[h*tok:(h+1)*tok,:hd]=hi
            qs[h*tok:(h+1)*tok,hd:]=(qf-hi.astype(jnp.float32)).astype(jnp.bfloat16)
        else:
            qs[h*tok:(h+1)*tok,:]=q
    for j in range(npage):
        src=pl.ds(pl.multiple_of(pages[j]*page,page),page)
        kb[j*page:(j+1)*page,:]=kp_ref[src,:]
        vb[j*page:(j+1)*page,:]=vp_ref[src,:]
    def block(k, v, first, mask_from):
        if wide: k=jnp.concatenate([k,k],axis=1)
        n=k.shape[0]
        for r in range(0,R,rt):
            rows=slice(r,r+rt)
            s=lax.dot_general(qs[rows,:],k,(((1,),(1,)),((),())),preferred_element_type=jnp.float32)
            if not wide: s=s*c
            if mask_from is not None:
                qpos=my*tok+lax.rem(lax.broadcasted_iota(jnp.int32,(rt,n),0)+r,tok)
                kpos=mask_from+lax.broadcasted_iota(jnp.int32,(rt,n),1)
                s=jnp.where(kpos<=qpos,s,-1e30)
            peak=jnp.max(s,axis=1,keepdims=True)
            if first:
                now=jnp.broadcast_to(peak,(rt,128))
            else:
                old=top[rows,:]
                now=jnp.maximum(old,peak)
            p=[jnp.exp2(s[:,i:i+128]-now) for i in range(0,n,128)]
            part=functools.reduce(jnp.add,p)
            pv=jnp.dot(jnp.concatenate([x.astype(jnp.bfloat16) for x in p],axis=1),v,preferred_element_type=jnp.float32)
            top[rows,:]=now
            if first:
                tot[rows,:]=part; acc[rows,:]=pv
            else:
                al=jnp.exp2(old-now)
                tot[rows,:]=tot[rows,:]*al+part
                acc[rows,:]=acc[rows,:]*al+pv
    npre=npage*page
    for i in range(0,npre,blk):
        block(kb[i:i+blk,:],vb[i:i+blk,:],i==0,None)
    end=(my+1)*tok
    full=lax.div(my*tok,blk)
    def step(i,_):
        at=pl.ds(pl.multiple_of(i*blk,blk),blk)
        block(ks_ref[at,:],vs_ref[at,:],False,None)
        return 0
    lax.fori_loop(0,full,step,0)
    at=pl.ds(pl.multiple_of(full*blk,blk),blk)
    block(ks_ref[at,:],vs_ref[at,:],False,full*blk)
    for h in range(share):
        rows=slice(h*tok,(h+1)*tok)
        l=jnp.sum(tot[rows,:],axis=1,keepdims=True)
        o_ref[:,h*hd:(h+1)*hd]=(acc[rows,:]/l).astype(jnp.bfloat16)

def flash(place,pages,q,page_rows,suffix,first_head,heads,kvh,share,hd,page,npage,blk=512,rt=1024,wide=False):
    tok=q.shape[0]
    total=suffix.shape[0]
    R=share*tok
    kv_cols=page_rows.shape[1]//(2*hd)
    body=functools.partial(flash_body,share=share,hd=hd,page=page,npage=npage,tok=tok,blk=blk,rt=rt,wide=wide)
    full=lambda n: (n,hd)
    return pl.pallas_call(body,
      out_shape=jax.ShapeDtypeStruct((tok,heads*share*hd),jnp.bfloat16),
      grid_spec=pltpu.PrefetchScalarGridSpec(num_scalar_prefetch=2,grid=(heads,),
        in_specs=[pl.BlockSpec((tok,share*hd),lambda g,*_:(0,first_head+g)),
          pl.BlockSpec((page_rows.shape[0],hd),lambda g,*_:(0,g)),
          pl.BlockSpec((page_rows.shape[0],hd),lambda g,*_:(0,kv_cols+g)),
          pl.BlockSpec((total,hd),lambda g,*_:(0,g)),
          pl.BlockSpec((total,hd),lambda g,*_:(0,kv_cols+g))],
        out_specs=pl.BlockSpec((tok,share*hd),lambda g,*_:(0,g)),
        scratch_shapes=[pltpu.VMEM((R,hd*(2 if wide else 1)),jnp.bfloat16),pltpu.VMEM((npage*page,hd),jnp.bfloat16),pltpu.VMEM((npage*page,hd),jnp.bfloat16),
          pltpu.VMEM((R,128),jnp.float32),pltpu.VMEM((R,128),jnp.float32),pltpu.VMEM((R,hd),jnp.float32)]),
      compiler_params=pltpu.CompilerParams(vmem_limit_bytes=50<<20,dimension_semantics=("arbitrary",)),
    )(place,pages,q,page_rows,page_rows,suffix,suffix)


def page_places(hit_owner):
    owners = hit_owner[:, 0]
    before = jnp.tril(jnp.ones((owners.shape[0],) * 2, jnp.int32), -1)
    rank = jnp.sum(before * (owners[None, :] == owners[:, None]), axis=1)
    return (owners * MOST + rank).astype(jnp.int32)


def body(query_rows, suffix_kv, delta_codes, anchors, scales, anchor_pos, hit_slot, hit_owner):
    my_index = lax.axis_index("pool")
    head_dim = query_rows.shape[1] // H
    page_len = delta_codes.shape[1]
    pages_now, _ = local_pages(
        delta_codes, anchors, scales, anchor_pos, hit_slot, hit_owner, my_index
    )
    width = suffix_kv.shape[1]
    page_rows = pages_now.reshape(MOST * page_len, width)
    mine = jnp.concatenate([page_rows, suffix_kv], axis=0)
    everyone = lax.all_gather(mine, "pool", axis=0)
    pages_all = everyone[:, : MOST * page_len].reshape(-1, width)
    suffix_all = everyone[:, MOST * page_len :].reshape(-1, width)
    place = my_index.astype(jnp.int32).reshape(1)
    return flash(place, page_places(hit_owner), query_rows, pages_all, suffix_all, 0, KVH, KVH,
                 H // KVH, head_dim, page_len, hit_slot.shape[0])


def solution(mesh):
    placed = (
        P(("groups", "pool"), None),
        P(("groups", "pool"), None),
        P(("groups", "pool"), None, None),
        P(("groups", "pool"), None),
        P(("groups", "pool"), None),
        P(("groups", "pool")),
        P("groups", None),
        P("groups", None),
    )
    return jax.shard_map(
        body, mesh=mesh, in_specs=placed, out_specs=P(("groups", "pool"), None), check_vma=False
    )
```

```python
import functools
import jax
import jax.numpy as jnp
from jax import lax
from jax.experimental import pallas as pl
from jax.experimental.pallas import tpu as pltpu
from jax.sharding import PartitionSpec as P

H = 64
KVH = 8
MOST = 6

LOG2E = 1.4426950408889634


def expand_pages(page_codes, page_anchor, page_scale, page_anchor_pos):
    page_len = page_codes.shape[1]
    head_dim = page_codes.shape[2] // page_scale.shape[1]
    triangle = (jnp.arange(page_len)[None, :] <= jnp.arange(page_len)[:, None]).astype(jnp.float32)
    anchor_row = jnp.take(triangle, page_anchor_pos, axis=0)
    mixing = triangle[None, :, :] - anchor_row[:, None, :]
    summed = jnp.einsum(
        "pts,psc->ptc", mixing, page_codes.astype(jnp.float32), precision=lax.Precision.HIGHEST
    )
    widened = jnp.repeat(page_scale, head_dim, axis=1)
    return (page_anchor.astype(jnp.float32)[:, None, :] + widened[:, None, :] * summed).astype(
        jnp.bfloat16
    )


def local_pages(delta_codes, anchors, scales, anchor_pos, hit_slot, hit_owner, my_index):
    owners = hit_owner[:, 0]
    slot_ids = hit_slot[:, 0]
    mine = (owners == my_index).astype(jnp.int32)
    page_rank = jnp.cumsum(mine) - 1
    buffer_ids = jnp.arange(MOST, dtype=jnp.int32)
    chosen = ((mine[None, :] == 1) & (page_rank[None, :] == buffer_ids[:, None])).astype(jnp.int32)
    picked = jnp.sum(chosen * slot_ids[None, :], axis=1)
    filled = jnp.sum(chosen, axis=1) > 0
    pages_now = expand_pages(
        jnp.take(delta_codes, picked, axis=0),
        jnp.take(anchors, picked, axis=0),
        jnp.take(scales, picked, axis=0),
        jnp.take(anchor_pos, picked, axis=0),
    )
    return (pages_now, filled)


PLANE = 4
MESH = pl.DeviceIdType.MESH


def gather_kernel(count, chunks, page_rows, mine, out, z_sem, y_sem, c_sem, got, own_sem):
    me = lax.axis_index("pool")
    levels = count // PLANE
    z = lax.div(me, PLANE)
    y = lax.rem(lax.div(me, 2), 2)
    c = lax.rem(me, 2)
    y_step = 2 - 4 * y
    y_peer, c_peer = me + y_step, me + 1 - 2 * c
    rows, width = mine.shape
    part = width // chunks

    def cut(k):
        return slice(k * part, (k + 1) * part)

    def send(own, owner, height, k, target, sem):
        area = (slice(0, height), cut(k))
        source = mine.at[area] if own else out.at[(owner,) + area]
        return pltpu.make_async_remote_copy(
            src_ref=source, dst_ref=out.at[(owner,) + area], send_sem=sem,
            recv_sem=got.at[k, owner], device_id={"pool": target}, device_id_type=MESH)

    def each(base, action):
        action(0, base, rows)
        for step in range(1, levels):
            @pl.when(z - step >= 0)
            def _():
                action(step, base - PLANE * step, rows)

            @pl.when(z + step < levels)
            def _():
                action(levels - 1 + step, base + PLANE * step, page_rows)

    def z_sends(k, action):
        for step in range(1, levels):
            @pl.when(z + step < levels)
            def _():
                action(send(True, me, rows, k, me + PLANE * step, z_sem.at[k, step - 1]))

            @pl.when(z - step >= 0)
            def _():
                action(send(True, me, page_rows, k, me - PLANE * step,
                            z_sem.at[k, levels - 2 + step]))

    barrier = pltpu.get_barrier_semaphore()
    for peer in (y_peer, c_peer):
        pl.semaphore_signal(barrier, inc=1, device_id={"pool": peer}, device_id_type=MESH)
    for step in range(1, levels):
        other = lax.rem(me + PLANE * step, count)
        pl.semaphore_signal(barrier, inc=1, device_id={"pool": other}, device_id_type=MESH)
    pl.semaphore_wait(barrier, levels + 1)

    kept = pltpu.make_async_copy(mine, out.at[me], own_sem)
    kept.start()
    for k in range(chunks):
        send(True, me, rows, k, y_peer, y_sem.at[k, 0]).start()
        z_sends(k, lambda copy: copy.start())
        send(True, me, rows, k, c_peer, c_sem.at[k, 0]).start()

    last = 2 * levels - 1

    def pass_column(k):
        def action(slot, owner, height):
            if slot == 0:
                return
            send(False, owner, height, k, y_peer, y_sem.at[k, slot]).wait_recv()
            send(False, owner, height, k, y_peer, y_sem.at[k, slot]).start()
            send(False, owner, height, k, c_peer, c_sem.at[k, slot]).start()
        each(me, action)

    def pass_side(k):
        def action(slot, owner, height):
            copy = send(False, owner, height, k, c_peer, c_sem.at[k, last + slot])
            copy.wait_recv()
            copy.start()
        each(y_peer, action)

    for k in range(chunks):
        pass_column(k)
        if k:
            pass_side(k - 1)
    pass_side(chunks - 1)

    for k in range(chunks):
        def landed(slot, owner, height):
            send(False, owner, height, k, c_peer, c_sem.at[k, slot]).wait_recv()
        each(c_peer, landed)
        each(c_peer + y_step, landed)
        z_sends(k, lambda copy: copy.wait_send())

        def left(slot, owner, height):
            send(slot == 0, owner, height, k, y_peer, y_sem.at[k, slot]).wait_send()
            send(slot == 0, owner, height, k, c_peer, c_sem.at[k, slot]).wait_send()
        each(me, left)

        def left_side(slot, owner, height):
            send(False, owner, height, k, c_peer, c_sem.at[k, last + slot]).wait_send()
        each(y_peer, left_side)
    kept.wait()


def gather_all(mine, count, page_rows, chunks=4):
    rows, width = mine.shape
    levels = count // PLANE
    dma = pltpu.SemaphoreType.DMA
    return pl.pallas_call(
        functools.partial(gather_kernel, count, chunks, page_rows),
        out_shape=jax.ShapeDtypeStruct((count, rows, width), mine.dtype),
        in_specs=[pl.BlockSpec(memory_space=pl.ANY)],
        out_specs=pl.BlockSpec(memory_space=pl.ANY),
        scratch_shapes=[dma((chunks, 2 * levels - 2)), dma((chunks, 2 * levels - 1)),
                        dma((chunks, 4 * levels - 2)), dma((chunks, count)), dma(())],
        compiler_params=pltpu.CompilerParams(collective_id=0, has_side_effects=True),
    )(mine)


def flash_body(place, pages, q_ref, k_ref, v_ref, o_ref, qs, kb, vb, top, tot, acc, *, share, hd, page, npage, tok, blk, rt, wide):
    my = place[0]
    R = share*tok
    c = hd**-0.5*LOG2E
    for h in range(share):
        q=q_ref[:, h*hd:(h+1)*hd]
        if wide:
            qf=q.astype(jnp.float32)*c
            hi=qf.astype(jnp.bfloat16)
            qs[h*tok:(h+1)*tok,:hd]=hi
            qs[h*tok:(h+1)*tok,hd:]=(qf-hi.astype(jnp.float32)).astype(jnp.bfloat16)
        else:
            qs[h*tok:(h+1)*tok,:]=q
    for j in range(npage):
        owner, rank = lax.div(pages[j], MOST), lax.rem(pages[j], MOST)
        src=pl.ds(pl.multiple_of(rank*page,page),page)
        kb[j*page:(j+1)*page,:]=k_ref[owner,src,:]
        vb[j*page:(j+1)*page,:]=v_ref[owner,src,:]
    def block(k, v, first, mask_from):
        if wide: k=jnp.concatenate([k,k],axis=1)
        n=k.shape[0]
        for r in range(0,R,rt):
            rows=slice(r,r+rt)
            s=lax.dot_general(qs[rows,:],k,(((1,),(1,)),((),())),preferred_element_type=jnp.float32)
            if not wide: s=s*c
            if mask_from is not None:
                qpos=my*tok+lax.rem(lax.broadcasted_iota(jnp.int32,(rt,n),0)+r,tok)
                kpos=mask_from+lax.broadcasted_iota(jnp.int32,(rt,n),1)
                s=jnp.where(kpos<=qpos,s,-1e30)
            peak=jnp.max(s,axis=1,keepdims=True)
            if first:
                now=jnp.broadcast_to(peak,(rt,128))
            else:
                old=top[rows,:]
                now=jnp.maximum(old,peak)
            p=[jnp.exp2(s[:,i:i+128]-now) for i in range(0,n,128)]
            part=functools.reduce(jnp.add,p)
            pv=jnp.dot(jnp.concatenate([x.astype(jnp.bfloat16) for x in p],axis=1),v,preferred_element_type=jnp.float32)
            top[rows,:]=now
            if first:
                tot[rows,:]=part; acc[rows,:]=pv
            else:
                al=jnp.exp2(old-now)
                tot[rows,:]=tot[rows,:]*al+part
                acc[rows,:]=acc[rows,:]*al+pv
    npre=npage*page
    for i in range(0,npre,blk):
        block(kb[i:i+blk,:],vb[i:i+blk,:],i==0,None)
    full=lax.div(my*tok,blk)
    head_rows, per = MOST*page, blk//tok
    def suffix(ref,i):
        return ref[pl.ds(i*per,per),head_rows:,:].reshape(blk,hd)
    def step(i,_):
        block(suffix(k_ref,i),suffix(v_ref,i),False,None)
        return 0
    lax.fori_loop(0,full,step,0)
    block(suffix(k_ref,full),suffix(v_ref,full),False,full*blk)
    for h in range(share):
        rows=slice(h*tok,(h+1)*tok)
        l=jnp.sum(tot[rows,:],axis=1,keepdims=True)
        o_ref[:,h*hd:(h+1)*hd]=(acc[rows,:]/l).astype(jnp.bfloat16)

def flash(place,pages,q,everyone,first_head,heads,kvh,share,hd,page,npage,blk=512,rt=1024,wide=False):
    tok=q.shape[0]
    count,all_rows=everyone.shape[:2]
    R=share*tok
    kv_cols=everyone.shape[2]//(2*hd)
    body=functools.partial(flash_body,share=share,hd=hd,page=page,npage=npage,tok=tok,blk=blk,rt=rt,wide=wide)
    return pl.pallas_call(body,
      out_shape=jax.ShapeDtypeStruct((tok,heads*share*hd),jnp.bfloat16),
      grid_spec=pltpu.PrefetchScalarGridSpec(num_scalar_prefetch=2,grid=(heads,),
        in_specs=[pl.BlockSpec((tok,share*hd),lambda g,*_:(0,first_head+g)),
          pl.BlockSpec((count,all_rows,hd),lambda g,*_:(0,0,g)),
          pl.BlockSpec((count,all_rows,hd),lambda g,*_:(0,0,kv_cols+g))],
        out_specs=pl.BlockSpec((tok,share*hd),lambda g,*_:(0,g)),
        scratch_shapes=[pltpu.VMEM((R,hd*(2 if wide else 1)),jnp.bfloat16),pltpu.VMEM((npage*page,hd),jnp.bfloat16),pltpu.VMEM((npage*page,hd),jnp.bfloat16),
          pltpu.VMEM((R,128),jnp.float32),pltpu.VMEM((R,128),jnp.float32),pltpu.VMEM((R,hd),jnp.float32)]),
      compiler_params=pltpu.CompilerParams(vmem_limit_bytes=50<<20,dimension_semantics=("arbitrary",)),
    )(place,pages,q,everyone,everyone)


def page_places(hit_owner):
    owners = hit_owner[:, 0]
    before = jnp.tril(jnp.ones((owners.shape[0],) * 2, jnp.int32), -1)
    rank = jnp.sum(before * (owners[None, :] == owners[:, None]), axis=1)
    return (owners * MOST + rank).astype(jnp.int32)


def body(query_rows, suffix_kv, delta_codes, anchors, scales, anchor_pos, hit_slot, hit_owner):
    my_index = lax.axis_index("pool")
    head_dim = query_rows.shape[1] // H
    page_len = delta_codes.shape[1]
    pages_now, _ = local_pages(
        delta_codes, anchors, scales, anchor_pos, hit_slot, hit_owner, my_index
    )
    width = suffix_kv.shape[1]
    page_rows = pages_now.reshape(MOST * page_len, width)
    mine = jnp.concatenate([page_rows, suffix_kv], axis=0)
    everyone = gather_all(mine, lax.axis_size("pool"), MOST * page_len)
    place = my_index.astype(jnp.int32).reshape(1)
    return flash(place, page_places(hit_owner), query_rows, everyone, 0, KVH, KVH,
                 H // KVH, head_dim, page_len, hit_slot.shape[0])


def solution(mesh):
    placed = (
        P(("groups", "pool"), None),
        P(("groups", "pool"), None),
        P(("groups", "pool"), None, None),
        P(("groups", "pool"), None),
        P(("groups", "pool"), None),
        P(("groups", "pool")),
        P("groups", None),
        P("groups", None),
    )
    return jax.shard_map(
        body, mesh=mesh, in_specs=placed, out_specs=P(("groups", "pool"), None), check_vma=False
    )
```

```python
import functools
import jax
import jax.numpy as jnp
from jax import lax
from jax.experimental import pallas as pl
from jax.experimental.pallas import tpu as pltpu
from jax.sharding import PartitionSpec as P

H = 64
KVH = 8
MOST = 6

LOG2E = 1.4426950408889634


def expand_pages(page_codes, page_anchor, page_scale, page_anchor_pos):
    page_len = page_codes.shape[1]
    head_dim = page_codes.shape[2] // page_scale.shape[1]
    triangle = (jnp.arange(page_len)[None, :] <= jnp.arange(page_len)[:, None]).astype(jnp.float32)
    anchor_row = jnp.take(triangle, page_anchor_pos, axis=0)
    mixing = triangle[None, :, :] - anchor_row[:, None, :]
    summed = jnp.einsum(
        "pts,psc->ptc", mixing, page_codes.astype(jnp.float32), precision=lax.Precision.HIGHEST
    )
    widened = jnp.repeat(page_scale, head_dim, axis=1)
    return (page_anchor.astype(jnp.float32)[:, None, :] + widened[:, None, :] * summed).astype(
        jnp.bfloat16
    )


def local_pages(delta_codes, anchors, scales, anchor_pos, hit_slot, hit_owner, my_index):
    owners = hit_owner[:, 0]
    slot_ids = hit_slot[:, 0]
    mine = (owners == my_index).astype(jnp.int32)
    page_rank = jnp.cumsum(mine) - 1
    buffer_ids = jnp.arange(MOST, dtype=jnp.int32)
    chosen = ((mine[None, :] == 1) & (page_rank[None, :] == buffer_ids[:, None])).astype(jnp.int32)
    picked = jnp.sum(chosen * slot_ids[None, :], axis=1)
    filled = jnp.sum(chosen, axis=1) > 0
    pages_now = expand_pages(
        jnp.take(delta_codes, picked, axis=0),
        jnp.take(anchors, picked, axis=0),
        jnp.take(scales, picked, axis=0),
        jnp.take(anchor_pos, picked, axis=0),
    )
    return (pages_now, filled)


PLANE = 4
MESH = pl.DeviceIdType.MESH


def attend_head(my, head, at, heads, pick_ref, q_ref, kv, o_ref, qs, kb, vb, top, tot, acc, *, share, page, blk=512):
    R, hd = qs.shape
    tok = R // share
    npre = kb.shape[0]
    c = hd**-0.5 * LOG2E
    k_cols = pl.ds(pl.multiple_of(at * hd, hd), hd)
    v_cols = pl.ds(pl.multiple_of((heads + at) * hd, hd), hd)

    def q_cols(h):
        return pl.ds(pl.multiple_of((head * share + h) * hd, hd), hd)

    for h in range(share):
        qs[h * tok : (h + 1) * tok, :] = q_ref[:, q_cols(h)]
    stored = jnp.concatenate([kv[:, 0 : MOST * page, k_cols], kv[:, 0 : MOST * page, v_cols]], axis=2)
    stored = stored.reshape(-1, 2 * hd)
    for i in range(0, npre, blk):
        hits = jnp.dot(pick_ref[i : i + blk, :], stored, preferred_element_type=jnp.float32)
        hits = hits.astype(jnp.bfloat16)
        kb[i : i + blk, :] = hits[:, :hd]
        vb[i : i + blk, :] = hits[:, hd:]

    def block(k, v, first, mask_from):
        n = k.shape[0]
        s = lax.dot_general(qs[...], k, (((1,), (1,)), ((), ())), preferred_element_type=jnp.float32) * c
        if mask_from is not None:
            qpos = my * tok + lax.rem(lax.broadcasted_iota(jnp.int32, (R, n), 0), tok)
            kpos = mask_from + lax.broadcasted_iota(jnp.int32, (R, n), 1)
            s = jnp.where(kpos <= qpos, s, -1e30)
        peak = jnp.max(s, axis=1, keepdims=True)
        if first:
            now = jnp.broadcast_to(peak, (R, 128))
        else:
            old = top[...]
            now = jnp.maximum(old, peak)
        p = [jnp.exp2(s[:, i : i + 128] - now) for i in range(0, n, 128)]
        part = functools.reduce(jnp.add, p)
        pv = jnp.dot(jnp.concatenate([x.astype(jnp.bfloat16) for x in p], axis=1), v,
                     preferred_element_type=jnp.float32)
        top[...] = now
        if first:
            tot[...] = part
            acc[...] = pv
        else:
            al = jnp.exp2(old - now)
            tot[...] = tot[...] * al + part
            acc[...] = acc[...] * al + pv

    for i in range(0, npre, blk):
        block(kb[i : i + blk, :], vb[i : i + blk, :], i == 0, None)
    full = lax.div(my * tok, blk)
    head_rows, per = MOST * page, blk // tok

    def suffix(cols, i):
        return kv[pl.ds(i * per, per), head_rows:, cols].reshape(blk, hd)

    def step(i, carry):
        block(suffix(k_cols, i), suffix(v_cols, i), False, None)
        return carry

    lax.fori_loop(0, full, step, 0)
    block(suffix(k_cols, full), suffix(v_cols, full), False, full * blk)
    for h in range(share):
        rows = slice(h * tok, (h + 1) * tok)
        l = jnp.sum(tot[rows, :], axis=1, keepdims=True)
        o_ref[:, q_cols(h)] = (acc[rows, :] / l).astype(jnp.bfloat16)


def fused_kernel(count, chunks, page_rows, share, page, pick_ref, q_ref, mine, o_ref, z_sem, y_sem, c_sem,
                 got, own_sem, qs, kb, vb, top, tot, acc, *out):
    me = lax.axis_index("pool")
    levels = count // PLANE
    z = lax.div(me, PLANE)
    y = lax.rem(lax.div(me, 2), 2)
    c = lax.rem(me, 2)
    y_step = 2 - 4 * y
    y_peer, c_peer = me + y_step, me + 1 - 2 * c
    rows = mine.shape[1]

    def send(own, owner, height, k, target, sem):
        place = out[k].at[owner, 0:height]
        source = mine.at[k, 0:height] if own else place
        return pltpu.make_async_remote_copy(
            src_ref=source, dst_ref=place, send_sem=sem,
            recv_sem=got.at[k, owner], device_id={"pool": target}, device_id_type=MESH)

    def each(base, action):
        action(0, base, rows)
        for step in range(1, levels):
            @pl.when(z - step >= 0)
            def _():
                action(step, base - PLANE * step, rows)

            @pl.when(z + step < levels)
            def _():
                action(levels - 1 + step, base + PLANE * step, page_rows)

    def z_sends(k, action):
        for step in range(1, levels):
            @pl.when(z + step < levels)
            def _():
                action(send(True, me, rows, k, me + PLANE * step, z_sem.at[k, step - 1]))

            @pl.when(z - step >= 0)
            def _():
                action(send(True, me, page_rows, k, me - PLANE * step,
                            z_sem.at[k, levels - 2 + step]))

    barrier = pltpu.get_barrier_semaphore()
    for peer in (y_peer, c_peer):
        pl.semaphore_signal(barrier, inc=1, device_id={"pool": peer}, device_id_type=MESH)
    for step in range(1, levels):
        other = lax.rem(me + PLANE * step, count)
        pl.semaphore_signal(barrier, inc=1, device_id={"pool": other}, device_id_type=MESH)
    pl.semaphore_wait(barrier, levels + 1)

    kept = [pltpu.make_async_copy(mine.at[k], out[k].at[me], own_sem.at[k]) for k in range(chunks)]
    for copy in kept:
        copy.start()
    for k in range(chunks):
        send(True, me, rows, k, y_peer, y_sem.at[k, 0]).start()
        z_sends(k, lambda copy: copy.start())
        send(True, me, rows, k, c_peer, c_sem.at[k, 0]).start()

    last = 2 * levels - 1

    def pass_column(k):
        def action(slot, owner, height):
            if slot == 0:
                return
            send(False, owner, height, k, y_peer, y_sem.at[k, slot]).wait_recv()
            send(False, owner, height, k, y_peer, y_sem.at[k, slot]).start()
            send(False, owner, height, k, c_peer, c_sem.at[k, slot]).start()
        each(me, action)

    def pass_side(k):
        def action(slot, owner, height):
            copy = send(False, owner, height, k, c_peer, c_sem.at[k, last + slot])
            copy.wait_recv()
            copy.start()
        each(y_peer, action)

    def arrive(k):
        def landed(slot, owner, height):
            send(False, owner, height, k, c_peer, c_sem.at[k, slot]).wait_recv()
        each(c_peer, landed)
        each(c_peer + y_step, landed)
        kept[k].wait()

    def attend(k):
        heads = mine.shape[2] // (2 * qs.shape[1])

        def one(at, carry):
            attend_head(me, k * heads + at, at, heads, pick_ref, q_ref, out[k], o_ref,
                        qs, kb, vb, top, tot, acc, share=share, page=page)
            return carry
        lax.fori_loop(0, heads, one, 0)

    for k in range(chunks):
        pass_column(k)
        if k:
            pass_side(k - 1)
            arrive(k - 1)
            attend(k - 1)
    pass_side(chunks - 1)
    arrive(chunks - 1)
    attend(chunks - 1)

    for k in range(chunks):
        z_sends(k, lambda copy: copy.wait_send())

        def left(slot, owner, height):
            send(slot == 0, owner, height, k, y_peer, y_sem.at[k, slot]).wait_send()
            send(slot == 0, owner, height, k, c_peer, c_sem.at[k, slot]).wait_send()
        each(me, left)

        def left_side(slot, owner, height):
            send(False, owner, height, k, c_peer, c_sem.at[k, last + slot]).wait_send()
        each(y_peer, left_side)


def gather_attend(pick, query_rows, mine, count, page, head_dim):
    chunks, rows, width = mine.shape
    levels = count // PLANE
    share = H // KVH
    tall = share * query_rows.shape[0]
    dma = pltpu.SemaphoreType.DMA
    vmem = pl.BlockSpec(memory_space=pltpu.VMEM)
    return pl.pallas_call(
        functools.partial(fused_kernel, count, chunks, MOST * page, share, page),
        out_shape=jax.ShapeDtypeStruct(query_rows.shape, jnp.bfloat16),
        in_specs=[vmem, vmem, pl.BlockSpec(memory_space=pl.ANY)],
        out_specs=vmem,
        scratch_shapes=[dma((chunks, 2 * levels - 2)), dma((chunks, 2 * levels - 1)),
                        dma((chunks, 4 * levels - 2)), dma((chunks, count)), dma((chunks,)),
                        pltpu.VMEM((tall, head_dim), jnp.bfloat16),
                        pltpu.VMEM((pick.shape[0], head_dim), jnp.bfloat16),
                        pltpu.VMEM((pick.shape[0], head_dim), jnp.bfloat16),
                        pltpu.VMEM((tall, 128), jnp.float32), pltpu.VMEM((tall, 128), jnp.float32),
                        pltpu.VMEM((tall, head_dim), jnp.float32)]
        + [pltpu.VMEM((count, rows, width), mine.dtype)] * chunks,
        compiler_params=pltpu.CompilerParams(
            collective_id=0, has_side_effects=True, vmem_limit_bytes=56 << 20),
    )(pick, query_rows, mine)


def page_places(hit_owner):
    owners = hit_owner[:, 0]
    before = jnp.tril(jnp.ones((owners.shape[0],) * 2, jnp.int32), -1)
    rank = jnp.sum(before * (owners[None, :] == owners[:, None]), axis=1)
    return (owners * MOST + rank).astype(jnp.int32)


def body(query_rows, suffix_kv, delta_codes, anchors, scales, anchor_pos, hit_slot, hit_owner):
    my_index = lax.axis_index("pool")
    head_dim = query_rows.shape[1] // H
    page_len = delta_codes.shape[1]
    pages_now, _ = local_pages(
        delta_codes, anchors, scales, anchor_pos, hit_slot, hit_owner, my_index
    )
    width = suffix_kv.shape[1]
    page_rows = pages_now.reshape(MOST * page_len, width)
    mine = jnp.concatenate([page_rows, suffix_kv], axis=0)
    chunks = 4
    mine = mine.reshape(mine.shape[0], 2, chunks, width // (2 * chunks)).transpose(2, 0, 1, 3)
    mine = mine.reshape(chunks, -1, width // chunks)
    count = lax.axis_size("pool")
    wanted = page_places(hit_owner)[:, None] * page_len + jnp.arange(page_len, dtype=jnp.int32)
    stored = jnp.arange(count * MOST * page_len, dtype=jnp.int32)
    pick = (wanted.reshape(-1, 1) == stored[None, :]).astype(jnp.bfloat16)
    return gather_attend(pick, query_rows, mine, count,
                         page_len, head_dim)


def solution(mesh):
    placed = (
        P(("groups", "pool"), None),
        P(("groups", "pool"), None),
        P(("groups", "pool"), None, None),
        P(("groups", "pool"), None),
        P(("groups", "pool"), None),
        P(("groups", "pool")),
        P("groups", None),
        P("groups", None),
    )
    return jax.shard_map(
        body, mesh=mesh, in_specs=placed, out_specs=P(("groups", "pool"), None), check_vma=False
    )
```
